768 devices in a mesh: ver: 2 (over z_hi), fsdp: 48 (over y, z_lo), tp: 8 (over x, core).
Axes of the slice: x: 4, y: 8, z: 12 (z_hi: 2, z_lo: 6; z = z_hi * 6 + z_lo), core: 2. Of those that a mesh axis runs over, the one named last changes fastest.
Arguments:
- train_acts: bfloat16 [2, 96, 128, 8192], P('ver', 'fsdp', None, 'tp'), may hold values from -6 to 6
- train_grads: bfloat16 [2, 96, 128, 24576], P('ver', 'fsdp', None, 'tp'), may hold values from -6 to 6
- query_acts: bfloat16 [2, 48, 128, 8192], P('ver', 'fsdp', None, 'tp'), may hold values from -6 to 6
- query_grads: bfloat16 [2, 48, 128, 24576], P('ver', 'fsdp', None, 'tp'), may hold values from -6 to 6
- proj_in: bfloat16 [64, 8192], P(None, 'tp'), may hold values from -0.0625 to 0.0625
- proj_out: bfloat16 [64, 24576], P(None, ('tp', 'fsdp')), may hold values from -0.0390625 to 0.0390625
- step_sizes: float32 [2], P('ver'), may hold values from 0.5 to 2
Outputs:
- influence: float32 [96, 48], P('fsdp')
The draws below stay inside these ranges and needn't reach their ends.
All inputs are finite; a program needn't handle non-finite values.
Results may differ from the reference program's by a relative error of at most 0.0003.
Values may be sent and summed in bfloat16 or wider, within the bound.
A program may use at most 32 MiB of HBM per device.

```python
import math
import jax
import jax.numpy as jnp
from jax import lax

D = 8192
FFW = 24576
RANK = 64
SEQ = 128
VERSIONS = 2
TRAIN = 96
QUERIES = 48


def levels(key, shape, pieces, least, high):
    def one(axis_at, shards_of):
        draws = jax.random.uniform(jax.random.fold_in(jax.random.fold_in(key, 6), axis_at), (shards_of,), jnp.float32, least / len(pieces), high / len(pieces))
        return jnp.repeat(jnp.exp(draws), shape[axis_at] // shards_of).reshape((-1,) + (1,) * (len(shape) - axis_at - 1))

    factor_of = one(*pieces[0])
    for cut in pieces[1:]:
        factor_of = factor_of * one(*cut)
    return factor_of


def scatter_about(rng, shape, deviation, most, pieces=(), dtype=jnp.bfloat16):
    loudness = levels(rng, shape, pieces, -0.22, 0.18) if pieces else 1.0
    array = jax.random.normal(rng, shape, jnp.float32) * deviation * loudness
    return jnp.minimum(jnp.maximum(array, -most), most).astype(dtype)


def setup_inputs(seed: int = 0) -> dict:
    splits = jax.random.split(jax.random.key(seed), 8)
    return {
        "train_acts": scatter_about(splits[0], (VERSIONS, TRAIN, SEQ, D), 1.0, 6.0, ((0, 2), (1, 48), (3, 8))),
        "train_grads": scatter_about(splits[1], (VERSIONS, TRAIN, SEQ, FFW), 1.0, 6.0, ((0, 2), (1, 48), (3, 8))),
        "query_acts": scatter_about(splits[2], (VERSIONS, QUERIES, SEQ, D), 1.0, 6.0, ((0, 2), (1, 48), (3, 8))),
        "query_grads": scatter_about(splits[3], (VERSIONS, QUERIES, SEQ, FFW), 1.0, 6.0, ((0, 2), (1, 48), (3, 8))),
        "proj_in": scatter_about(splits[4], (RANK, D), D ** -0.5, 0.0625, ((1, 8),)),
        "proj_out": scatter_about(splits[5], (RANK, FFW), FFW ** -0.5, 0.0390625, ((1, 384),)),
        "step_sizes": jnp.clip(jnp.exp(math.log(2.0) - 1.3862944 * jax.random.uniform(splits[6], (VERSIONS,), jnp.float32) ** levels(splits[6], (VERSIONS,), ((0, 2),), -0.2, 0.2)), 0.5, 2.0),
    }


def sequence_grads(acts, outgrads, proj_in, proj_out):
    count, length, width_in = acts.shape
    inputs = jnp.dot(acts.reshape(count * length, width_in), proj_in.T, preferred_element_type=jnp.float32)
    outputs = jnp.dot(outgrads.reshape(count * length, outgrads.shape[2]), proj_out.T, preferred_element_type=jnp.float32)
    inputs = inputs.reshape(count, length, RANK)
    outputs = outputs.reshape(count, length, RANK)
    return jnp.einsum("nsa,nsb->nab", inputs, outputs, precision=lax.Precision.HIGHEST) / SEQ


def reference(train_acts, train_grads, query_acts, query_grads, proj_in, proj_out, step_sizes):
    influence = jnp.zeros((TRAIN, QUERIES), jnp.float32)
    for version in range(VERSIONS):
        train_part = sequence_grads(train_acts[version], train_grads[version], proj_in, proj_out)
        query_part = sequence_grads(query_acts[version], query_grads[version], proj_in, proj_out)
        gram_part = jnp.dot(train_part.reshape(TRAIN, RANK * RANK), query_part.reshape(QUERIES, RANK * RANK).T, precision=lax.Precision.HIGHEST)
        influence = influence + step_sizes[version] * gram_part
    return influence
```

```python
import functools

import jax
import jax.numpy as jnp
from jax import lax
from jax.experimental import pallas as pl
from jax.experimental.pallas import tpu as pltpu
from jax.sharding import PartitionSpec as P

NZ = 6
MESH = pl.DeviceIdType.MESH
F32 = jnp.float32
BF16 = jnp.bfloat16
NT = (((1,), (1,)), ((), ()))


def split(x):
    hi = x.astype(BF16)
    return hi, (x - hi.astype(F32)).astype(BF16)


def kernel(
    nver, ny, ntp,
    train_acts, train_grads, query_acts, query_grads, proj_in, proj_out, step,
    out,
    acts, grads, pin, pout, pbuf, at_part, at_recv, at_full, bsum, gp, grecv, zq, crow, dbuf,
    load_sem, pz_recv, pr_recv, pl_recv, p_send, ring_send,
    a_send, a_recv, ag_send, ag_recv, g_send, g_recv, z_send, z_recv, y_send, y_recv, d_send, d_recv,
):
    ver = lax.axis_index("ver")
    fsdp = lax.axis_index("fsdp")
    tp = lax.axis_index("tp")
    y, z = fsdp // NZ, fsdp % NZ
    half = NZ // 2
    trains, queries = train_acts.shape[1], query_acts.shape[1]
    count = trains + queries
    seq = train_acts.shape[2]
    tokens = count * seq

    def at_z(d):
        return {"fsdp": y * NZ + (z + d) % NZ}

    def at_y(d):
        return {"fsdp": ((y + d) % ny) * NZ + z}

    def at_tp(d):
        return {"tp": (tp + d) % ntp}

    def at_ver(v, d):
        return {"ver": (ver + v) % nver, "tp": (tp + d) % ntp}

    def push(src, dst, send, recv, where):
        copy = pltpu.make_async_remote_copy(
            src_ref=src, dst_ref=dst, send_sem=send, recv_sem=recv, device_id=where, device_id_type=MESH
        )
        copy.start()

    def wait(ref, sem):
        pltpu.make_async_copy(ref, ref, sem).wait()

    load_pout = pltpu.make_async_copy(proj_out, pout, load_sem.at[0])
    load_pout.start()
    barrier = pltpu.get_barrier_semaphore()
    partners = [at_y(d) for d in range(1, ny)] + [at_z(d) for d in range(1, NZ)] + [at_tp(d) for d in range(1, ntp)]
    partners += [at_ver(v, d) for v in range(1, nver) for d in range(ntp)]
    for where in partners:
        pl.semaphore_signal(barrier, inc=1, device_id=where, device_id_type=MESH)
    loads_a = [
        pltpu.make_async_copy(proj_in, pin, load_sem.at[1]),
        pltpu.make_async_copy(train_acts.at[0], acts.at[pl.ds(0, trains)], load_sem.at[2]),
        pltpu.make_async_copy(query_acts.at[0], acts.at[pl.ds(trains, queries)], load_sem.at[3]),
    ]
    loads_g = [
        pltpu.make_async_copy(train_grads.at[0], grads.at[pl.ds(0, trains)], load_sem.at[4]),
        pltpu.make_async_copy(query_grads.at[0], grads.at[pl.ds(trains, queries)], load_sem.at[5]),
    ]
    for load in loads_a + loads_g:
        load.start()

    load_pout.wait()
    own = pout[...].astype(F32)
    rank = own.shape[0]
    pbuf[y, z] = jnp.concatenate([own[: rank // 2], own[rank // 2 :]], axis=1).astype(BF16)

    pl.semaphore_wait(barrier, len(partners))
    for d in range(1, NZ):
        push(pbuf.at[y, z], pbuf.at[y, z], p_send, pz_recv.at[z], at_z(d))

    for load in loads_a:
        load.wait()
    a_part = lax.dot_general(pin[...], acts[...].reshape(tokens, -1), NT, preferred_element_type=F32)
    at_part[...] = a_part.reshape(at_part.shape)
    for d in range(1, ntp):
        push(at_part.at[(tp + d) % ntp], at_recv.at[d - 1], a_send, a_recv, at_tp(d))

    first = z // half
    chunks = (first, 1 - first)
    hops_right = (ny // 2, ny // 2 - 1)
    hops_left = (ny // 2 - 1, ny // 2)

    def send_right(s, k):
        row = (y + ny - s) % ny
        part = pbuf.at[row, pl.ds(chunks[k] * half, half)]
        push(part, part, ring_send, pr_recv.at[s * 2 + k], at_y(1))

    def send_left(s, k):
        row = (y + s) % ny
        part = pbuf.at[row, pl.ds(chunks[k] * half, half)]
        push(part, part, ring_send, pl_recv.at[s * 2 + k], at_y(ny - 1))

    lane = lax.broadcasted_iota(jnp.int32, (rank // 2, 2 * rank), 1)
    is_left = lane < rank

    def add_row(row, start):
        cols = []
        for p in range(half):
            even = pbuf[row, 2 * p].astype(F32)
            odd = pbuf[row, 2 * p + 1].astype(F32)
            low = jnp.where(is_left, even, pltpu.roll(odd, rank, 1)).astype(BF16)
            high = jnp.where(is_left, pltpu.roll(even, rank, 1), odd).astype(BF16)
            cols.append(jnp.concatenate([low, high, low, high], axis=0))
        width = NZ * rank
        g = grads[:, :, pl.ds(pl.multiple_of(row * width, 128), width)].reshape(tokens, width)
        term = lax.dot_general(g, jnp.concatenate(cols, axis=1), NT, preferred_element_type=F32)
        if start:
            bsum[...] = term
        else:
            bsum[...] += term

    one_block = pbuf.at[0, 0]
    one_chunk = pbuf.at[0, pl.ds(0, half)]
    for k in range(2):
        if k == 0:
            others = [first * half + (z % half + i) % half for i in range(1, half)]
        else:
            others = [(1 - first) * half + i for i in range(half)]
        for other in others:
            wait(one_block, pz_recv.at[other])
        if hops_right[k] > 0:
            send_right(0, k)
        if hops_left[k] > 0:
            send_left(0, k)
    for load in loads_g:
        load.wait()
    add_row(y, True)

    wait(at_recv, a_recv)
    mine = at_part[tp]
    for d in range(ntp - 1):
        mine = mine + at_recv[d]
    at_full[tp] = mine
    for d in range(1, ntp):
        push(at_full.at[tp], at_full.at[tp], ag_send, ag_recv, at_tp(d))

    for s in range(1, ny // 2 + 1):
        for k in range(2):
            if s - 1 < hops_right[k]:
                wait(one_chunk, pr_recv.at[(s - 1) * 2 + k])
                if s < hops_right[k]:
                    send_right(s, k)
            if s - 1 < hops_left[k]:
                wait(one_chunk, pl_recv.at[(s - 1) * 2 + k])
                if s < hops_left[k]:
                    send_left(s, k)
        add_row((y + ny - s) % ny, False)
        if s < ny // 2:
            add_row((y + s) % ny, False)

    wait(at_full.at[pl.ds(0, ntp - 1)], ag_recv)
    lanes2 = lax.broadcasted_iota(jnp.int32, (seq, 2 * rank), 1) < rank
    rows = rank // 2 // ntp
    for n in range(count):
        at = at_full[:, :, n * seq : (n + 1) * seq].reshape(rank, seq)
        a_hi, a_lo = split(jnp.concatenate([at[: rank // 2], at[rank // 2 :]], axis=1))
        b = bsum[n * seq : (n + 1) * seq, :]
        b_hi, b_lo = split(jnp.concatenate([jnp.where(lanes2, b, 0.0), jnp.where(lanes2, 0.0, b)], axis=0))
        both = jnp.dot(jnp.concatenate([a_hi, a_lo], axis=0), b_hi, preferred_element_type=F32)
        grad = both[: rank // 2] + (both[rank // 2 :] + jnp.dot(a_hi, b_lo, preferred_element_type=F32))
        for t in range(ntp):
            gp[t, n * rows : (n + 1) * rows, :] = grad[t * rows : (t + 1) * rows, :]
    for d in range(1, ntp):
        push(gp.at[(tp + d) % ntp], grecv.at[d - 1], g_send, g_recv, at_tp(d))
    wait(grecv, g_recv)
    grad = gp[tp]
    for d in range(ntp - 1):
        grad = grad + grecv[d]

    zq[z] = grad[trains * rows :, :]
    for d in range(1, NZ):
        push(zq.at[z], zq.at[z], z_send, z_recv, at_z(d))
    wait(zq.at[pl.ds(0, NZ - 1)], z_recv)
    for k in range(NZ):
        crow[y, k * rows : (k + 1) * rows, :] = zq[k]
    for d in range(1, ny):
        push(crow.at[y], crow.at[y], y_send, y_recv, at_y(d))
    wait(crow.at[pl.ds(0, ny - 1)], y_recv)

    wide = ny * NZ * rows
    q_hi, q_lo = split(crow[...].reshape(wide, 2 * rank))
    t_hi, t_lo = split(grad[: trains * rows, :])
    many = trains * rows
    both = lax.dot_general(jnp.concatenate([t_hi, t_lo], axis=0), q_hi, NT, preferred_element_type=F32)
    cross = both[:many] + (both[many:] + lax.dot_general(t_hi, q_lo, NT, preferred_element_type=F32))
    row_id = lax.broadcasted_iota(jnp.int32, (many, wide), 0) % rows
    col_id = lax.broadcasted_iota(jnp.int32, (many, wide), 1) % rows
    cross = jnp.where(row_id == col_id, cross, 0.0)
    c_hi, c_rest = cross.astype(BF16), cross
    c_rest = c_rest - c_hi.astype(F32)
    c_mid, c_lo = split(c_rest)
    pick_from = lax.broadcasted_iota(jnp.int32, (wide, 128), 0) // rows
    pick_to = lax.broadcasted_iota(jnp.int32, (wide, 128), 1)
    pick = jnp.where(pick_from == pick_to, 1.0, 0.0).astype(BF16)
    three = jnp.dot(jnp.concatenate([c_hi, c_mid, c_lo], axis=0), pick, preferred_element_type=F32)
    part = three[:many] + (three[many : 2 * many] + three[2 * many :])
    me = ver * ntp + tp
    dbuf[me] = part * (step[0] / (seq * seq))

    for v in reversed(range(nver)):
        for d in range(ntp):
            if v or d:
                push(dbuf.at[me], dbuf.at[me], d_send, d_recv, at_ver(v, d))
    wait(dbuf.at[pl.ds(0, nver * ntp - 1)], d_recv)
    total = dbuf[0]
    for i in range(1, nver * ntp):
        total = total + dbuf[i]
    width = out.shape[1]
    for n in range(trains):
        out[n : n + 1, :] = jnp.sum(total[n * rows : (n + 1) * rows, :], axis=0, keepdims=True)[:, :width]

    wait(pbuf.at[0, pl.ds(0, NZ - 1)], p_send)
    wait(pbuf.at[pl.ds(0, ny - 1)], ring_send)
    wait(at_recv, a_send)
    wait(at_recv, ag_send)
    wait(grecv, g_send)
    wait(zq.at[pl.ds(0, NZ - 1)], z_send)
    wait(crow.at[pl.ds(0, ny - 1)], y_send)
    wait(dbuf.at[pl.ds(0, nver * ntp - 1)], d_send)


def solution(mesh):
    nver, nfsdp, ntp = mesh.shape["ver"], mesh.shape["fsdp"], mesh.shape["tp"]
    ny = nfsdp // NZ

    def body(train_acts, train_grads, query_acts, query_grads, proj_in, proj_out, step_sizes):
        rank, din = proj_in.shape
        trains, queries = train_acts.shape[1], query_acts.shape[1]
        count, seq = trains + queries, train_acts.shape[2]
        tokens, dout = count * seq, train_grads.shape[3]
        arows = rank // ntp
        rows = rank // 2 // ntp
        dma = pltpu.SemaphoreType.DMA
        hbm = pl.BlockSpec(memory_space=pl.ANY)
        return pl.pallas_call(
            functools.partial(kernel, nver, ny, ntp),
            out_shape=jax.ShapeDtypeStruct((trains, nfsdp * queries), F32),
            in_specs=[hbm] * 6 + [pl.BlockSpec(memory_space=pltpu.SMEM)],
            out_specs=pl.BlockSpec(memory_space=pltpu.VMEM),
            scratch_shapes=[
                pltpu.VMEM((count, seq, din), BF16),
                pltpu.VMEM((count, seq, dout), BF16),
                pltpu.VMEM((rank, din), BF16),
                pltpu.VMEM(proj_out.shape, BF16),
                pltpu.VMEM((ny, NZ, rank // 2, 2 * proj_out.shape[1]), BF16),
                pltpu.VMEM((ntp, arows, tokens), F32),
                pltpu.VMEM((ntp - 1, arows, tokens), F32),
                pltpu.VMEM((ntp, arows, tokens), F32),
                pltpu.VMEM((tokens, 2 * rank), F32),
                pltpu.VMEM((ntp, count * rows, 2 * rank), F32),
                pltpu.VMEM((ntp - 1, count * rows, 2 * rank), F32),
                pltpu.VMEM((NZ, rows, 2 * rank), F32),
                pltpu.VMEM((ny, NZ * rows, 2 * rank), F32),
                pltpu.VMEM((nver * ntp, trains * rows, 128), F32),
                dma((6,)), dma((NZ,)), dma((ny,)), dma((ny,)), dma, dma,
                dma, dma, dma, dma, dma, dma, dma, dma, dma, dma, dma, dma,
            ],
            compiler_params=pltpu.CompilerParams(
                collective_id=0, has_side_effects=True, vmem_limit_bytes=40 * 1024 * 1024
            ),
        )(train_acts, train_grads, query_acts, query_grads, proj_in, proj_out, step_sizes)

    in_specs = (
        P("ver", "fsdp", None, "tp"),
        P("ver", "fsdp", None, "tp"),
        P("ver", "fsdp", None, "tp"),
        P("ver", "fsdp", None, "tp"),
        P(None, "tp"),
        P(None, ("tp", "fsdp")),
        P("ver"),
    )
    return jax.shard_map(body, mesh=mesh, in_specs=in_specs, out_specs=P("fsdp", None), check_vma=False)
```

```python
import functools

import jax
import jax.numpy as jnp
from jax import lax
from jax.experimental import pallas as pl
from jax.experimental.pallas import tpu as pltpu
from jax.sharding import PartitionSpec as P

NZ = 6
MESH = pl.DeviceIdType.MESH
F32 = jnp.float32
BF16 = jnp.bfloat16
NT = (((1,), (1,)), ((), ()))


def split(x):
    hi = x.astype(BF16)
    return hi, (x - hi.astype(F32)).astype(BF16)


def kernel(
    nver, ny, ntp,
    train_acts, train_grads, query_acts, query_grads, proj_in, proj_out, step,
    out,
    acts, grads, pin, pout, pbuf, at_part, at_recv, at_full, bsum, gp, grecv, zq, crow, dbuf,
    load_sem, pz_recv, py_recv, pz_send, py_send,
    a_send, a_recv, ag_send, ag_recv, g_send, g_recv, z_send, z_recv, y_send, y_recv, d_send, d_recv,
):
    ver = lax.axis_index("ver")
    fsdp = lax.axis_index("fsdp")
    tp = lax.axis_index("tp")
    y, z = lax.div(fsdp, NZ), lax.rem(fsdp, NZ)
    half = NZ // 2
    trains, queries = train_acts.shape[1], query_acts.shape[1]
    count = trains + queries
    seq = train_acts.shape[2]
    tokens = count * seq

    def at_z(zz):
        return {"fsdp": y * NZ + zz}

    def at_y(d):
        return {"fsdp": lax.rem(y + d, ny) * NZ + z}

    def at_tp(d):
        return {"tp": lax.rem(tp + d, ntp)}

    def at_ver(v, d):
        return {"ver": lax.rem(ver + v, nver), "tp": lax.rem(tp + d, ntp)}

    tp_order = sorted(range(1, ntp), key=lambda d: abs(d - ntp // 2))
    y_order = sorted(range(1, ny), key=lambda d: abs(d - ny // 2))
    ver_order = [(v, d) for v in range(1, nver) for d in tp_order + [0]]
    zhalf, zpos = lax.div(z, half), lax.rem(z, half)
    other_z = [(1 - zhalf) * half + j for j in range(half)]
    same_z = [zhalf * half + lax.rem(zpos + i, half) for i in range(1, half)]

    def push(src, dst, send, recv, where):
        copy = pltpu.make_async_remote_copy(
            src_ref=src, dst_ref=dst, send_sem=send, recv_sem=recv, device_id=where, device_id_type=MESH
        )
        copy.start()

    def wait(ref, sem):
        pltpu.make_async_copy(ref, ref, sem).wait()

    load_pout = pltpu.make_async_copy(proj_out, pout, load_sem.at[0])
    load_pout.start()
    barrier = pltpu.get_barrier_semaphore()
    partners = [at_ver(v, d) for v, d in ver_order]
    partners += [at_y(d) for d in y_order[:1]] + [at_z(zz) for zz in other_z] + [at_y(d) for d in y_order[1:3]]
    partners += [at_tp(d) for d in tp_order[:3]] + [at_y(d) for d in y_order[3:]] + [at_z(zz) for zz in same_z]
    partners += [at_tp(d) for d in tp_order[3:]]
    for where in partners:
        pl.semaphore_signal(barrier, inc=1, device_id=where, device_id_type=MESH)
    loads_a = [
        pltpu.make_async_copy(proj_in, pin, load_sem.at[1]),
        pltpu.make_async_copy(train_acts.at[0], acts.at[pl.ds(0, trains)], load_sem.at[2]),
        pltpu.make_async_copy(query_acts.at[0], acts.at[pl.ds(trains, queries)], load_sem.at[3]),
    ]
    loads_g = [
        pltpu.make_async_copy(train_grads.at[0], grads.at[pl.ds(0, trains)], load_sem.at[4]),
        pltpu.make_async_copy(query_grads.at[0], grads.at[pl.ds(trains, queries)], load_sem.at[5]),
    ]
    for load in loads_a + loads_g:
        load.start()

    load_pout.wait()
    own = pout[...].astype(F32)
    rank = own.shape[0]
    pbuf[y, 0] = jnp.concatenate([own[: rank // 2], own[rank // 2 :]], axis=1).astype(BF16)

    pl.semaphore_wait(barrier, len(partners))
    pieces = (pl.ds(0, 1), pl.ds(1, half - 1), pl.ds(half, half))

    def push_row(piece):
        for d in y_order:
            push(pbuf.at[y, piece], pbuf.at[y, piece], py_send, py_recv.at[d], at_y(d))

    for zz in other_z:
        push(pbuf.at[y, 0], pbuf.at[y, half + zpos], pz_send, pz_recv.at[1], at_z(zz))
    for i, zz in enumerate(same_z):
        push(pbuf.at[y, 0], pbuf.at[y, half - 1 - i], pz_send, pz_recv.at[0], at_z(zz))
    push_row(pieces[0])

    for load in loads_a:
        load.wait()
    a_part = lax.dot_general(pin[...], acts[...].reshape(tokens, -1), NT, preferred_element_type=F32)
    at_part[...] = a_part.reshape(at_part.shape)
    for d in tp_order:
        push(at_part.at[(tp + d) % ntp], at_recv.at[d - 1], a_send, a_recv, at_tp(d))

    lane = lax.broadcasted_iota(jnp.int32, (rank // 2, 2 * rank), 1)
    is_left = lane < rank
    slots = [
        jnp.where(k // half == zhalf, lax.rem(k % half - zpos + half, half), half + k % half) for k in range(NZ)
    ]

    def add_row(row, start):
        cols = []
        for p in range(half):
            even = pbuf[row, slots[2 * p]].astype(F32)
            odd = pbuf[row, slots[2 * p + 1]].astype(F32)
            low = jnp.where(is_left, even, pltpu.roll(odd, rank, 1)).astype(BF16)
            high = jnp.where(is_left, pltpu.roll(even, rank, 1), odd).astype(BF16)
            cols.append(jnp.concatenate([low, high, low, high], axis=0))
        width = NZ * rank
        g = grads[:, :, pl.ds(pl.multiple_of(row * width, 128), width)].reshape(tokens, width)
        term = lax.dot_general(g, jnp.concatenate(cols, axis=1), NT, preferred_element_type=F32)
        if start:
            bsum[...] = term
        else:
            bsum[...] += term

    for piece, sem in ((pieces[1], 0), (pieces[2], 1)):
        wait(pbuf.at[y, piece], pz_recv.at[sem])
        push_row(piece)
    for load in loads_g:
        load.wait()
    add_row(y, True)

    wait(at_recv, a_recv)
    mine = at_part[tp]
    for d in range(ntp - 1):
        mine = mine + at_recv[d]
    at_full[tp] = mine
    for d in tp_order:
        push(at_full.at[tp], at_full.at[tp], ag_send, ag_recv, at_tp(d))

    for d in reversed(y_order):
        row = lax.rem(y + ny - d, ny)
        wait(pbuf.at[row], py_recv.at[d])
        add_row(row, False)

    wait(at_full.at[pl.ds(0, ntp - 1)], ag_recv)
    lanes2 = lax.broadcasted_iota(jnp.int32, (seq, 2 * rank), 1) < rank
    rows = rank // 2 // ntp
    for n in range(count):
        at = at_full[:, :, n * seq : (n + 1) * seq].reshape(rank, seq)
        a_hi, a_lo = split(jnp.concatenate([at[: rank // 2], at[rank // 2 :]], axis=1))
        b = bsum[n * seq : (n + 1) * seq, :]
        b_hi, b_lo = split(jnp.concatenate([jnp.where(lanes2, b, 0.0), jnp.where(lanes2, 0.0, b)], axis=0))
        both = jnp.dot(jnp.concatenate([a_hi, a_lo], axis=0), b_hi, preferred_element_type=F32)
        grad = both[: rank // 2] + (both[rank // 2 :] + jnp.dot(a_hi, b_lo, preferred_element_type=F32))
        for t in range(ntp):
            gp[t, n * rows : (n + 1) * rows, :] = grad[t * rows : (t + 1) * rows, :]
    for d in tp_order:
        push(gp.at[(tp + d) % ntp], grecv.at[d - 1], g_send, g_recv, at_tp(d))
    wait(grecv, g_recv)
    grad = gp[tp]
    for d in range(ntp - 1):
        grad = grad + grecv[d]

    zq[z] = grad[trains * rows :, :]
    for zz in other_z + same_z:
        push(zq.at[z], zq.at[z], z_send, z_recv, at_z(zz))
    wait(zq.at[pl.ds(0, NZ - 1)], z_recv)
    for k in range(NZ):
        crow[y, k * rows : (k + 1) * rows, :] = zq[k]
    for d in y_order:
        push(crow.at[y], crow.at[y], y_send, y_recv, at_y(d))
    wait(crow.at[pl.ds(0, ny - 1)], y_recv)

    wide = ny * NZ * rows
    q_hi, q_lo = split(crow[...].reshape(wide, 2 * rank))
    t_hi, t_lo = split(grad[: trains * rows, :])
    many = trains * rows
    both = lax.dot_general(jnp.concatenate([t_hi, t_lo], axis=0), q_hi, NT, preferred_element_type=F32)
    cross = both[:many] + (both[many:] + lax.dot_general(t_hi, q_lo, NT, preferred_element_type=F32))
    row_id = lax.broadcasted_iota(jnp.int32, (many, wide), 0) % rows
    col_id = lax.broadcasted_iota(jnp.int32, (many, wide), 1) % rows
    cross = jnp.where(row_id == col_id, cross, 0.0)
    c_hi, c_rest = cross.astype(BF16), cross
    c_rest = c_rest - c_hi.astype(F32)
    c_mid, c_lo = split(c_rest)
    pick_from = lax.broadcasted_iota(jnp.int32, (wide, 128), 0) // rows
    pick_to = lax.broadcasted_iota(jnp.int32, (wide, 128), 1)
    pick = jnp.where(pick_from == pick_to, 1.0, 0.0).astype(BF16)
    three = jnp.dot(jnp.concatenate([c_hi, c_mid, c_lo], axis=0), pick, preferred_element_type=F32)
    part = three[:many] + (three[many : 2 * many] + three[2 * many :])
    me = ver * ntp + tp
    dbuf[me] = part * (step[0] / (seq * seq))

    for v, d in ver_order + [(0, d) for d in tp_order]:
        push(dbuf.at[me], dbuf.at[me], d_send, d_recv, at_ver(v, d))
    wait(dbuf.at[pl.ds(0, nver * ntp - 1)], d_recv)
    total = dbuf[0]
    for i in range(1, nver * ntp):
        total = total + dbuf[i]
    width = out.shape[1]
    for n in range(trains):
        out[n : n + 1, :] = jnp.sum(total[n * rows : (n + 1) * rows, :], axis=0, keepdims=True)[:, :width]

    wait(pbuf.at[0, pl.ds(0, NZ - 1)], pz_send)
    wait(pbuf.at[pl.ds(0, ny - 1)], py_send)
    wait(at_recv, a_send)
    wait(at_recv, ag_send)
    wait(grecv, g_send)
    wait(zq.at[pl.ds(0, NZ - 1)], z_send)
    wait(crow.at[pl.ds(0, ny - 1)], y_send)
    wait(dbuf.at[pl.ds(0, nver * ntp - 1)], d_send)


def solution(mesh):
    nver, nfsdp, ntp = mesh.shape["ver"], mesh.shape["fsdp"], mesh.shape["tp"]
    ny = nfsdp // NZ

    def body(train_acts, train_grads, query_acts, query_grads, proj_in, proj_out, step_sizes):
        rank, din = proj_in.shape
        trains, queries = train_acts.shape[1], query_acts.shape[1]
        count, seq = trains + queries, train_acts.shape[2]
        tokens, dout = count * seq, train_grads.shape[3]
        arows = rank // ntp
        rows = rank // 2 // ntp
        dma = pltpu.SemaphoreType.DMA
        hbm = pl.BlockSpec(memory_space=pl.ANY)
        return pl.pallas_call(
            functools.partial(kernel, nver, ny, ntp),
            out_shape=jax.ShapeDtypeStruct((trains, nfsdp * queries), F32),
            in_specs=[hbm] * 6 + [pl.BlockSpec(memory_space=pltpu.SMEM)],
            out_specs=pl.BlockSpec(memory_space=pltpu.VMEM),
            scratch_shapes=[
                pltpu.VMEM((count, seq, din), BF16),
                pltpu.VMEM((count, seq, dout), BF16),
                pltpu.VMEM((rank, din), BF16),
                pltpu.VMEM(proj_out.shape, BF16),
                pltpu.VMEM((ny, NZ, rank // 2, 2 * proj_out.shape[1]), BF16),
                pltpu.VMEM((ntp, arows, tokens), F32),
                pltpu.VMEM((ntp - 1, arows, tokens), F32),
                pltpu.VMEM((ntp, arows, tokens), F32),
                pltpu.VMEM((tokens, 2 * rank), F32),
                pltpu.VMEM((ntp, count * rows, 2 * rank), F32),
                pltpu.VMEM((ntp - 1, count * rows, 2 * rank), F32),
                pltpu.VMEM((NZ, rows, 2 * rank), F32),
                pltpu.VMEM((ny, NZ * rows, 2 * rank), F32),
                pltpu.VMEM((nver * ntp, trains * rows, 128), F32),
                dma((6,)), dma((2,)), dma((ny,)), dma, dma,
                dma, dma, dma, dma, dma, dma, dma, dma, dma, dma, dma, dma,
            ],
            compiler_params=pltpu.CompilerParams(
                collective_id=0, has_side_effects=True, vmem_limit_bytes=60 * 1024 * 1024
            ),
        )(train_acts, train_grads, query_acts, query_grads, proj_in, proj_out, step_sizes)

    in_specs = (
        P("ver", "fsdp", None, "tp"),
        P("ver", "fsdp", None, "tp"),
        P("ver", "fsdp", None, "tp"),
        P("ver", "fsdp", None, "tp"),
        P(None, "tp"),
        P(None, ("tp", "fsdp")),
        P("ver"),
    )
    return jax.shard_map(body, mesh=mesh, in_specs=in_specs, out_specs=P("fsdp", None), check_vma=False)
```

```python
import functools

import jax
import jax.numpy as jnp
from jax import lax
from jax.experimental import pallas as pl
from jax.experimental.pallas import tpu as pltpu
from jax.sharding import PartitionSpec as P

NZ = 6
MESH = pl.DeviceIdType.MESH
F32 = jnp.float32
BF16 = jnp.bfloat16
NT = (((1,), (1,)), ((), ()))


def split(x):
    hi = x.astype(BF16)
    return hi, (x - hi.astype(F32)).astype(BF16)


def kernel(
    nver, ny, ntp,
    train_acts, train_grads, query_acts, query_grads, proj_in, proj_out, step_size,
    out,
    acts, grads, pin, pout, pbuf, at_part, at_recv, at_full, bsum, gp, grecv, qbuf, crow, dbuf, step,
    load_sem, p_sems, p_far, q_sems, q_far,
    a_send, a_recv, ag_send, ag_recv, g_send, g_recv, d_send, d_recv,
):
    ver = lax.axis_index("ver")
    fsdp = lax.axis_index("fsdp")
    tp = lax.axis_index("tp")
    y, z = lax.div(fsdp, NZ), lax.rem(fsdp, NZ)
    half = NZ // 2
    trains, queries = train_acts.shape[1], query_acts.shape[1]
    count = trains + queries
    seq = train_acts.shape[2]
    tokens = count * seq

    def at_z(zz):
        return {"fsdp": y * NZ + zz}

    def at_y(d):
        return {"fsdp": lax.rem(y + d, ny) * NZ + z}

    def at_tp(d):
        return {"tp": lax.rem(tp + d, ntp)}

    def at_ver(v, d):
        return {"ver": lax.rem(ver + v, nver), "tp": lax.rem(tp + d, ntp)}

    tp_order = sorted(range(1, ntp), key=lambda d: abs(d - ntp // 2))
    y_order = sorted(range(1, ny), key=lambda d: abs(d - ny // 2))
    ver_order = [(v, d) for v in range(1, nver) for d in tp_order + [0]]
    zhalf, zpos = lax.div(z, half), lax.rem(z, half)
    other_z = [(1 - zhalf) * half + j for j in range(half)]
    same_z = [zhalf * half + lax.rem(zpos + i, half) for i in range(1, half)]

    def push(src, dst, send, recv, where):
        copy = pltpu.make_async_remote_copy(
            src_ref=src, dst_ref=dst, send_sem=send, recv_sem=recv, device_id=where, device_id_type=MESH
        )
        copy.start()

    def wait(ref, sem):
        pltpu.make_async_copy(ref, ref, sem).wait()

    load_pout = pltpu.make_async_copy(proj_out, pout, load_sem.at[0])
    load_pout.start()
    barrier = pltpu.get_barrier_semaphore()
    partners = [at_z(zz) for zz in other_z] + [at_y(d) for d in y_order[:3]]
    partners += [at_ver(v, d) for v, d in ver_order] + [at_tp(d) for d in tp_order[:3]]
    partners += [at_y(d) for d in y_order[3:]] + [at_z(zz) for zz in same_z] + [at_tp(d) for d in tp_order[3:]]
    for where in partners:
        pl.semaphore_signal(barrier, inc=1, device_id=where, device_id_type=MESH)
    loads_a = [
        pltpu.make_async_copy(proj_in, pin, load_sem.at[1]),
        pltpu.make_async_copy(train_acts.at[0], acts.at[pl.ds(0, trains)], load_sem.at[2]),
        pltpu.make_async_copy(query_acts.at[0], acts.at[pl.ds(trains, queries)], load_sem.at[3]),
    ]
    loads_g = [
        pltpu.make_async_copy(train_grads.at[0], grads.at[pl.ds(0, trains)], load_sem.at[4]),
        pltpu.make_async_copy(query_grads.at[0], grads.at[pl.ds(trains, queries)], load_sem.at[5]),
    ]
    load_step = pltpu.make_async_copy(step_size, step, load_sem.at[6])
    for load in loads_a + loads_g + [load_step]:
        load.start()

    near, far = pl.ds(1, half - 1), pl.ds(half, half)

    def gather_own(buf, sems):
        for zz in other_z:
            push(buf.at[y, 0], buf.at[y, half + zpos], sems.at[0], sems.at[4], at_z(zz))
        for d in y_order:
            push(buf.at[y, 0], buf.at[y, 0], sems.at[1], sems.at[5], at_y(d))

    def gather_rest(buf, sems, far_recv):
        wait(buf.at[y, far], sems.at[4])
        for d in y_order:
            push(buf.at[y, far], buf.at[y, far], sems.at[3], far_recv.at[d], at_y(d))
        wait(buf.at[pl.ds(0, ny - 1), 0], sems.at[5])
        for i, zz in enumerate(same_z):
            push(buf.at[:, 0], buf.at[:, half - 1 - i], sems.at[2], sems.at[6], at_z(zz))

    def gather_sent(buf, sems):
        wait(buf.at[0, far], sems.at[0])
        wait(buf.at[pl.ds(0, ny - 1), 0], sems.at[1])
        wait(buf.at[:, near], sems.at[2])
        wait(buf.at[pl.ds(0, ny - 1), far], sems.at[3])

    slots = [
        jnp.where(k // half == zhalf, lax.rem(k % half - zpos + half, half), half + k % half) for k in range(NZ)
    ]

    load_pout.wait()
    own = pout[...].astype(F32)
    rank = own.shape[0]
    pbuf[y, 0] = jnp.concatenate([own[: rank // 2], own[rank // 2 :]], axis=1).astype(BF16)

    for load in loads_a:
        load.wait()
    a_part = lax.dot_general(pin[...], acts[...].reshape(tokens, -1), NT, preferred_element_type=F32)
    at_part[...] = a_part.reshape(at_part.shape)
    pl.semaphore_wait(barrier, len(partners))
    gather_own(pbuf, p_sems)

    for d in tp_order:
        push(at_part.at[(tp + d) % ntp], at_recv.at[d - 1], a_send, a_recv, at_tp(d))

    lane = lax.broadcasted_iota(jnp.int32, (rank // 2, 2 * rank), 1)
    is_left = lane < rank

    def add_row(row, start):
        cols = []
        for p in range(half):
            even = pbuf[row, slots[2 * p]].astype(F32)
            odd = pbuf[row, slots[2 * p + 1]].astype(F32)
            low = jnp.where(is_left, even, pltpu.roll(odd, rank, 1)).astype(BF16)
            high = jnp.where(is_left, pltpu.roll(even, rank, 1), odd).astype(BF16)
            cols.append(jnp.concatenate([low, high, low, high], axis=0))
        width = NZ * rank
        g = grads[:, :, pl.ds(pl.multiple_of(row * width, 128), width)].reshape(tokens, width)
        term = lax.dot_general(g, jnp.concatenate(cols, axis=1), NT, preferred_element_type=F32)
        if start:
            bsum[...] = term
        else:
            bsum[...] += term

    gather_rest(pbuf, p_sems, p_far)
    for load in loads_g + [load_step]:
        load.wait()
    wait(at_recv, a_recv)
    mine = at_part[tp]
    for d in range(ntp - 1):
        mine = mine + at_recv[d]
    at_full[tp] = mine
    for d in tp_order:
        push(at_full.at[tp], at_full.at[tp], ag_send, ag_recv, at_tp(d))

    wait(pbuf.at[:, near], p_sems.at[6])
    add_row(y, True)
    for d in reversed(y_order):
        row = lax.rem(y + ny - d, ny)
        wait(pbuf.at[row, far], p_far.at[d])
        add_row(row, False)

    wait(at_full.at[pl.ds(0, ntp - 1)], ag_recv)
    lanes2 = lax.broadcasted_iota(jnp.int32, (seq, 2 * rank), 1) < rank
    rows = rank // 2 // ntp
    for n in range(count):
        at = at_full[:, :, n * seq : (n + 1) * seq].reshape(rank, seq)
        a_hi, a_lo = split(jnp.concatenate([at[: rank // 2], at[rank // 2 :]], axis=1))
        b = bsum[n * seq : (n + 1) * seq, :]
        b_hi, b_lo = split(jnp.concatenate([jnp.where(lanes2, b, 0.0), jnp.where(lanes2, 0.0, b)], axis=0))
        both = jnp.dot(jnp.concatenate([a_hi, a_lo], axis=0), b_hi, preferred_element_type=F32)
        grad = both[: rank // 2] + (both[rank // 2 :] + jnp.dot(a_hi, b_lo, preferred_element_type=F32))
        for t in range(ntp):
            gp[t, n * rows : (n + 1) * rows, :] = grad[t * rows : (t + 1) * rows, :]
    for d in tp_order:
        push(gp.at[(tp + d) % ntp], grecv.at[d - 1], g_send, g_recv, at_tp(d))
    wait(grecv, g_recv)
    grad = gp[tp]
    for d in range(ntp - 1):
        grad = grad + grecv[d]

    qbuf[y, 0] = grad[trains * rows :, :]
    gather_own(qbuf, q_sems)
    gather_rest(qbuf, q_sems, q_far)
    wait(qbuf.at[:, near], q_sems.at[6])
    for d in [0] + y_order[::-1]:
        row = lax.rem(y + ny - d, ny)
        if d:
            wait(qbuf.at[row, far], q_far.at[d])
        for k in range(NZ):
            crow[row, k * rows : (k + 1) * rows, :] = qbuf[row, slots[k]]

    wide = ny * NZ * rows
    q_hi, q_lo = split(crow[...].reshape(wide, 2 * rank))
    t_hi, t_lo = split(grad[: trains * rows, :])
    many = trains * rows
    both = lax.dot_general(jnp.concatenate([t_hi, t_lo], axis=0), q_hi, NT, preferred_element_type=F32)
    cross = both[:many] + (both[many:] + lax.dot_general(t_hi, q_lo, NT, preferred_element_type=F32))
    row_id = lax.broadcasted_iota(jnp.int32, (many, wide), 0) % rows
    col_id = lax.broadcasted_iota(jnp.int32, (many, wide), 1) % rows
    cross = jnp.where(row_id == col_id, cross, 0.0)
    c_hi, c_rest = cross.astype(BF16), cross
    c_rest = c_rest - c_hi.astype(F32)
    c_mid, c_lo = split(c_rest)
    pick_from = lax.broadcasted_iota(jnp.int32, (wide, 128), 0) // rows
    pick_to = lax.broadcasted_iota(jnp.int32, (wide, 128), 1)
    pick = jnp.where(pick_from == pick_to, 1.0, 0.0).astype(BF16)
    three = jnp.dot(jnp.concatenate([c_hi, c_mid, c_lo], axis=0), pick, preferred_element_type=F32)
    part = three[:many] + (three[many : 2 * many] + three[2 * many :])
    me = ver * ntp + tp
    dbuf[me] = part * (step[0] / (seq * seq))

    targets = [{"ver": 0, "tp": lax.rem(tp + d, ntp)} for d in tp_order] + [at_ver(v, 0) for v in range(1, nver)]
    targets += [{"ver": v, "tp": lax.rem(tp + d, ntp)} for v in range(1, nver) for d in tp_order]
    for where in targets:
        push(dbuf.at[me], dbuf.at[me], d_send, d_recv, where)
    wait(dbuf.at[pl.ds(0, nver * ntp - 1)], d_recv)
    total = dbuf[0]
    for i in range(1, nver * ntp):
        total = total + dbuf[i]
    width = out.shape[1]
    for n in range(trains):
        out[n : n + 1, :] = jnp.sum(total[n * rows : (n + 1) * rows, :], axis=0, keepdims=True)[:, :width]

    gather_sent(pbuf, p_sems)
    gather_sent(qbuf, q_sems)
    wait(at_recv, a_send)
    wait(at_recv, ag_send)
    wait(grecv, g_send)
    wait(dbuf.at[pl.ds(0, nver * ntp - 1)], d_send)


def solution(mesh):
    nver, nfsdp, ntp = mesh.shape["ver"], mesh.shape["fsdp"], mesh.shape["tp"]
    ny = nfsdp // NZ

    def body(train_acts, train_grads, query_acts, query_grads, proj_in, proj_out, step_sizes):
        rank, din = proj_in.shape
        trains, queries = train_acts.shape[1], query_acts.shape[1]
        count, seq = trains + queries, train_acts.shape[2]
        tokens, dout = count * seq, train_grads.shape[3]
        arows = rank // ntp
        rows = rank // 2 // ntp
        dma = pltpu.SemaphoreType.DMA
        hbm = pl.BlockSpec(memory_space=pl.ANY)
        return pl.pallas_call(
            functools.partial(kernel, nver, ny, ntp),
            out_shape=jax.ShapeDtypeStruct((trains, nfsdp * queries), F32),
            in_specs=[hbm] * 7,
            out_specs=pl.BlockSpec(memory_space=pltpu.VMEM),
            scratch_shapes=[
                pltpu.VMEM((count, seq, din), BF16),
                pltpu.VMEM((count, seq, dout), BF16),
                pltpu.VMEM((rank, din), BF16),
                pltpu.VMEM(proj_out.shape, BF16),
                pltpu.VMEM((ny, NZ, rank // 2, 2 * proj_out.shape[1]), BF16),
                pltpu.VMEM((ntp, arows, tokens), F32),
                pltpu.VMEM((ntp - 1, arows, tokens), F32),
                pltpu.VMEM((ntp, arows, tokens), F32),
                pltpu.VMEM((tokens, 2 * rank), F32),
                pltpu.VMEM((ntp, count * rows, 2 * rank), F32),
                pltpu.VMEM((ntp - 1, count * rows, 2 * rank), F32),
                pltpu.VMEM((ny, NZ, rows, 2 * rank), F32),
                pltpu.VMEM((ny, NZ * rows, 2 * rank), F32),
                pltpu.VMEM((nver * ntp, trains * rows, 128), F32),
                pltpu.SMEM((1,), F32),
                dma((7,)), dma((7,)), dma((ny,)), dma((7,)), dma((ny,)),
                dma, dma, dma, dma, dma, dma, dma, dma,
            ],
            compiler_params=pltpu.CompilerParams(
                collective_id=0, has_side_effects=True, vmem_limit_bytes=56550000
            ),
        )(train_acts, train_grads, query_acts, query_grads, proj_in, proj_out, step_sizes)

    in_specs = (
        P("ver", "fsdp", None, "tp"),
        P("ver", "fsdp", None, "tp"),
        P("ver", "fsdp", None, "tp"),
        P("ver", "fsdp", None, "tp"),
        P(None, "tp"),
        P(None, ("tp", "fsdp")),
        P("ver"),
    )
    return jax.shard_map(body, mesh=mesh, in_specs=in_specs, out_specs=P("fsdp", None), check_vma=False)
```

```python
import functools

import jax
import jax.numpy as jnp
from jax import lax
from jax.experimental import pallas as pl
from jax.experimental.pallas import tpu as pltpu
from jax.sharding import PartitionSpec as P

NZ = 6
MESH = pl.DeviceIdType.MESH
F32 = jnp.float32
BF16 = jnp.bfloat16
NT = (((1,), (1,)), ((), ()))


def split(x):
    hi = x.astype(BF16)
    return hi, (x - hi.astype(F32)).astype(BF16)


def kernel(
    nver, ny, ntp,
    train_acts, train_grads, query_acts, query_grads, proj_in, proj_out, step_size,
    out,
    acts, grads, pin, pout, pbuf, at_part, at_recv, at_full, pfull, bsum, gp, grecv, gq, gqrecv, qbuf, crow, dbuf, step,
    load_sem, p_sems, p_far, q_sems, q_far,
    a_send, a_recv, ag_send, ag_recv, g_send, g_recv, gq_send, gq_recv, d_send, d_recv,
):
    ver = lax.axis_index("ver")
    fsdp = lax.axis_index("fsdp")
    tp = lax.axis_index("tp")
    y, z = lax.div(fsdp, NZ), lax.rem(fsdp, NZ)
    half = NZ // 2
    trains, queries = train_acts.shape[1], query_acts.shape[1]
    count = trains + queries
    seq = train_acts.shape[2]
    tokens = count * seq

    def at_z(zz):
        return {"fsdp": y * NZ + zz}

    def at_y(d):
        return {"fsdp": lax.rem(y + d, ny) * NZ + z}

    def at_tp(d):
        return {"tp": lax.rem(tp + d, ntp)}

    def at_ver(v, d):
        return {"ver": lax.rem(ver + v, nver), "tp": lax.rem(tp + d, ntp)}

    tp_order = sorted(range(1, ntp), key=lambda d: abs(d - ntp // 2))
    y_order = sorted(range(1, ny), key=lambda d: abs(d - ny // 2))
    ver_order = [(v, d) for v in range(1, nver) for d in tp_order + [0]]
    zhalf, zpos = lax.div(z, half), lax.rem(z, half)
    other_z = [(1 - zhalf) * half + j for j in range(half)]
    same_z = [zhalf * half + lax.rem(zpos + i, half) for i in range(1, half)]

    def push(src, dst, send, recv, where):
        copy = pltpu.make_async_remote_copy(
            src_ref=src, dst_ref=dst, send_sem=send, recv_sem=recv, device_id=where, device_id_type=MESH
        )
        copy.start()

    def wait(ref, sem):
        pltpu.make_async_copy(ref, ref, sem).wait()

    load_pout = pltpu.make_async_copy(proj_out, pout, load_sem.at[0])
    load_pout.start()
    barrier = pltpu.get_barrier_semaphore()
    partners = [at_z(zz) for zz in other_z] + [at_y(d) for d in y_order[:3]]
    partners += [at_ver(v, d) for v, d in ver_order] + [at_tp(d) for d in tp_order[:3]]
    partners += [at_y(d) for d in y_order[3:]] + [at_z(zz) for zz in same_z] + [at_tp(d) for d in tp_order[3:]]
    for where in partners:
        pl.semaphore_signal(barrier, inc=1, device_id=where, device_id_type=MESH)
    loads_a = [
        pltpu.make_async_copy(proj_in, pin, load_sem.at[1]),
        pltpu.make_async_copy(train_acts.at[0], acts.at[pl.ds(0, trains)], load_sem.at[2]),
        pltpu.make_async_copy(query_acts.at[0], acts.at[pl.ds(trains, queries)], load_sem.at[3]),
    ]
    loads_g = [
        pltpu.make_async_copy(train_grads.at[0], grads.at[pl.ds(0, trains)], load_sem.at[4]),
        pltpu.make_async_copy(query_grads.at[0], grads.at[pl.ds(trains, queries)], load_sem.at[5]),
    ]
    load_step = pltpu.make_async_copy(step_size, step, load_sem.at[6])
    for load in loads_a + loads_g + [load_step]:
        load.start()

    near, far = pl.ds(1, half - 1), pl.ds(half, half)
    opposite = lax.rem(y + ny // 2, ny)

    def gather_own(buf, sems, far_recv):
        for zz in other_z:
            push(buf.at[y, 0], buf.at[y, half + zpos], sems.at[0], sems.at[4], at_z(zz))
        for d in y_order:
            recv = far_recv.at[0] if d == y_order[0] else sems.at[5]
            push(buf.at[y, 0], buf.at[y, 0], sems.at[1], recv, at_y(d))

    def gather_rest(buf, sems, far_recv):
        wait(buf.at[opposite, 0], far_recv.at[0])
        for zz in other_z:
            push(buf.at[opposite, 0], buf.at[opposite, half + zpos], sems.at[0], far_recv.at[y_order[0]], at_z(zz))
        wait(buf.at[pl.ds(0, ny - 2), 0], sems.at[5])
        for i, zz in enumerate(same_z):
            push(buf.at[:, 0], buf.at[:, half - 1 - i], sems.at[2], sems.at[6], at_z(zz))
        wait(buf.at[y, far], sems.at[4])
        for d in y_order[1:]:
            push(buf.at[y, far], buf.at[y, far], sems.at[3], far_recv.at[d], at_y(d))

    def gather_sent(buf, sems):
        wait(buf.at[pl.ds(0, 2), far], sems.at[0])
        wait(buf.at[pl.ds(0, ny - 1), 0], sems.at[1])
        wait(buf.at[:, near], sems.at[2])
        wait(buf.at[pl.ds(0, ny - 2), far], sems.at[3])

    slots = [
        jnp.where(k // half == zhalf, lax.rem(k % half - zpos + half, half), half + k % half) for k in range(NZ)
    ]

    load_pout.wait()
    own = pout[...].astype(F32)
    rank = own.shape[0]
    pbuf[y, 0] = jnp.concatenate([own[: rank // 2], own[rank // 2 :]], axis=1).astype(BF16)

    for load in loads_a:
        load.wait()
    a_part = lax.dot_general(pin[...], acts[...].reshape(tokens, -1), NT, preferred_element_type=F32)
    at_part[...] = a_part.reshape(at_part.shape)
    pl.semaphore_wait(barrier, len(partners))
    gather_own(pbuf, p_sems, p_far)

    for d in tp_order:
        push(at_part.at[(tp + d) % ntp], at_recv.at[d - 1], a_send, a_recv, at_tp(d))

    lane = lax.broadcasted_iota(jnp.int32, (rank // 2, 2 * rank), 1)
    is_left = lane < rank

    def add_row(row, start):
        cols = []
        for p in range(half):
            even = pbuf[row, slots[2 * p]].astype(F32)
            odd = pbuf[row, slots[2 * p + 1]].astype(F32)
            low = jnp.where(is_left, even, pltpu.roll(odd, rank, 1)).astype(BF16)
            high = jnp.where(is_left, pltpu.roll(even, rank, 1), odd).astype(BF16)
            cols.append(jnp.concatenate([low, high, low, high], axis=0))
        width = NZ * rank
        columns = pl.ds(pl.multiple_of(row * width, 128), width)
        pfull[:, columns] = jnp.concatenate(cols, axis=1)
        g = grads[trains:, :, columns].reshape(queries * seq, width)
        term = lax.dot_general(g, pfull[:, columns], NT, preferred_element_type=F32)
        if start:
            bsum[trains * seq :, :] = term
        else:
            bsum[trains * seq :, :] += term

    gather_rest(pbuf, p_sems, p_far)
    for load in loads_g + [load_step]:
        load.wait()
    wait(at_recv, a_recv)
    mine = at_part[tp]
    for d in range(ntp - 1):
        mine = mine + at_recv[d]
    at_full[tp] = mine
    for d in tp_order:
        push(at_full.at[tp], at_full.at[tp], ag_send, ag_recv, at_tp(d))

    wait(pbuf.at[:, near], p_sems.at[6])
    add_row(y, True)
    for d in reversed(y_order):
        row = lax.rem(y + ny - d, ny)
        wait(pbuf.at[row, far], p_far.at[d])
        add_row(row, False)

    wait(at_full.at[pl.ds(0, ntp - 1)], ag_recv)
    lanes2 = lax.broadcasted_iota(jnp.int32, (seq, 2 * rank), 1) < rank
    rows = rank // 2 // ntp

    def grad_parts(n, parts, at_row):
        at = at_full[:, :, n * seq : (n + 1) * seq].reshape(rank, seq)
        a_hi, a_lo = split(jnp.concatenate([at[: rank // 2], at[rank // 2 :]], axis=1))
        b = bsum[n * seq : (n + 1) * seq, :]
        b_hi, b_lo = split(jnp.concatenate([jnp.where(lanes2, b, 0.0), jnp.where(lanes2, 0.0, b)], axis=0))
        both = jnp.dot(jnp.concatenate([a_hi, a_lo], axis=0), b_hi, preferred_element_type=F32)
        grad = both[: rank // 2] + (both[rank // 2 :] + jnp.dot(a_hi, b_lo, preferred_element_type=F32))
        for t in range(ntp):
            parts[t, at_row : at_row + rows, :] = grad[t * rows : (t + 1) * rows, :]

    grad_parts(trains, gq, 0)
    for d in tp_order:
        push(gq.at[lax.rem(tp + d, ntp)], gqrecv.at[d - 1], gq_send, gq_recv, at_tp(d))
    g = grads[:trains].reshape(trains * seq, -1)
    bsum[: trains * seq, :] = lax.dot_general(g, pfull[...], NT, preferred_element_type=F32)
    for n in range(trains):
        grad_parts(n, gp, n * rows)
    for d in tp_order:
        push(gp.at[lax.rem(tp + d, ntp)], grecv.at[d - 1], g_send, g_recv, at_tp(d))
    wait(gqrecv, gq_recv)
    query = gq[tp]
    for d in range(ntp - 1):
        query = query + gqrecv[d]

    qbuf[y, 0] = query
    gather_own(qbuf, q_sems, q_far)
    gather_rest(qbuf, q_sems, q_far)
    wait(grecv, g_recv)
    grad = gp[tp]
    for d in range(ntp - 1):
        grad = grad + grecv[d]
    wait(qbuf.at[:, near], q_sems.at[6])
    for d in [0] + y_order[::-1]:
        row = lax.rem(y + ny - d, ny)
        if d:
            wait(qbuf.at[row, far], q_far.at[d])
        for k in range(NZ):
            crow[row, k * rows : (k + 1) * rows, :] = qbuf[row, slots[k]]

    wide = ny * NZ * rows
    q_hi, q_lo = split(crow[...].reshape(wide, 2 * rank))
    t_hi, t_lo = split(grad)
    many = trains * rows
    both = lax.dot_general(jnp.concatenate([t_hi, t_lo], axis=0), q_hi, NT, preferred_element_type=F32)
    cross = both[:many] + (both[many:] + lax.dot_general(t_hi, q_lo, NT, preferred_element_type=F32))
    row_id = lax.broadcasted_iota(jnp.int32, (many, wide), 0) % rows
    col_id = lax.broadcasted_iota(jnp.int32, (many, wide), 1) % rows
    cross = jnp.where(row_id == col_id, cross, 0.0)
    c_hi, c_rest = cross.astype(BF16), cross
    c_rest = c_rest - c_hi.astype(F32)
    c_mid, c_lo = split(c_rest)
    pick_from = lax.broadcasted_iota(jnp.int32, (wide, 128), 0) // rows
    pick_to = lax.broadcasted_iota(jnp.int32, (wide, 128), 1)
    pick = jnp.where(pick_from == pick_to, 1.0, 0.0).astype(BF16)
    three = jnp.dot(jnp.concatenate([c_hi, c_mid, c_lo], axis=0), pick, preferred_element_type=F32)
    part = three[:many] + (three[many : 2 * many] + three[2 * many :])
    me = ver * ntp + tp
    dbuf[me] = part * (step[0] / (seq * seq))

    targets = [{"ver": 0, "tp": lax.rem(tp + d, ntp)} for d in tp_order] + [at_ver(v, 0) for v in range(1, nver)]
    targets += [{"ver": v, "tp": lax.rem(tp + d, ntp)} for v in range(1, nver) for d in tp_order]
    for where in targets:
        push(dbuf.at[me], dbuf.at[me], d_send, d_recv, where)
    wait(dbuf.at[pl.ds(0, nver * ntp - 1)], d_recv)
    total = dbuf[0]
    for i in range(1, nver * ntp):
        total = total + dbuf[i]
    width = out.shape[1]
    for n in range(trains):
        out[n : n + 1, :] = jnp.sum(total[n * rows : (n + 1) * rows, :], axis=0, keepdims=True)[:, :width]

    gather_sent(pbuf, p_sems)
    gather_sent(qbuf, q_sems)
    wait(at_recv, a_send)
    wait(at_recv, ag_send)
    wait(grecv, g_send)
    wait(gqrecv, gq_send)
    wait(dbuf.at[pl.ds(0, nver * ntp - 1)], d_send)


def solution(mesh):
    nver, nfsdp, ntp = mesh.shape["ver"], mesh.shape["fsdp"], mesh.shape["tp"]
    ny = nfsdp // NZ

    def body(train_acts, train_grads, query_acts, query_grads, proj_in, proj_out, step_sizes):
        rank, din = proj_in.shape
        trains, queries = train_acts.shape[1], query_acts.shape[1]
        count, seq = trains + queries, train_acts.shape[2]
        tokens, dout = count * seq, train_grads.shape[3]
        arows = rank // ntp
        rows = rank // 2 // ntp
        dma = pltpu.SemaphoreType.DMA
        hbm = pl.BlockSpec(memory_space=pl.ANY)
        return pl.pallas_call(
            functools.partial(kernel, nver, ny, ntp),
            out_shape=jax.ShapeDtypeStruct((trains, nfsdp * queries), F32),
            in_specs=[hbm] * 7,
            out_specs=pl.BlockSpec(memory_space=pltpu.VMEM),
            scratch_shapes=[
                pltpu.VMEM((count, seq, din), BF16),
                pltpu.VMEM((count, seq, dout), BF16),
                pltpu.VMEM((rank, din), BF16),
                pltpu.VMEM(proj_out.shape, BF16),
                pltpu.VMEM((ny, NZ, rank // 2, 2 * proj_out.shape[1]), BF16),
                pltpu.VMEM((ntp, arows, tokens), F32),
                pltpu.VMEM((ntp - 1, arows, tokens), F32),
                pltpu.VMEM((ntp, arows, tokens), F32),
                pltpu.VMEM((2 * rank, dout), BF16),
                pltpu.VMEM((tokens, 2 * rank), F32),
                pltpu.VMEM((ntp, trains * rows, 2 * rank), F32),
                pltpu.VMEM((ntp - 1, trains * rows, 2 * rank), F32),
                pltpu.VMEM((ntp, queries * rows, 2 * rank), F32),
                pltpu.VMEM((ntp - 1, queries * rows, 2 * rank), F32),
                pltpu.VMEM((ny, NZ, rows, 2 * rank), F32),
                pltpu.VMEM((ny, NZ * rows, 2 * rank), F32),
                pltpu.VMEM((nver * ntp, trains * rows, 128), F32),
                pltpu.SMEM((1,), F32),
                dma((7,)), dma((7,)), dma((ny,)), dma((7,)), dma((ny,)),
                dma, dma, dma, dma, dma, dma, dma, dma, dma, dma,
            ],
            compiler_params=pltpu.CompilerParams(
                collective_id=0, has_side_effects=True, vmem_limit_bytes=56550000
            ),
        )(train_acts, train_grads, query_acts, query_grads, proj_in, proj_out, step_sizes)

    in_specs = (
        P("ver", "fsdp", None, "tp"),
        P("ver", "fsdp", None, "tp"),
        P("ver", "fsdp", None, "tp"),
        P("ver", "fsdp", None, "tp"),
        P(None, "tp"),
        P(None, ("tp", "fsdp")),
        P("ver"),
    )
    return jax.shard_map(body, mesh=mesh, in_specs=in_specs, out_specs=P("fsdp", None), check_vma=False)
```

```python
import functools

import jax
import jax.numpy as jnp
from jax import lax
from jax.experimental import pallas as pl
from jax.experimental.pallas import tpu as pltpu
from jax.sharding import PartitionSpec as P

NZ = 6
MESH = pl.DeviceIdType.MESH
F32 = jnp.float32
BF16 = jnp.bfloat16
NT = (((1,), (1,)), ((), ()))


def split(x):
    hi = x.astype(BF16)
    return hi, (x - hi.astype(F32)).astype(BF16)


def kernel(
    nver, ny, ntp,
    train_acts, train_grads, query_acts, query_grads, proj_in, proj_out, step_size,
    out,
    acts, grads, pin, pout, pbuf, at_part, at_recv, at_full, pfull, bsum, gp, grecv, gq, gqrecv, qbuf, crow, dbuf, step,
    load_sem, p_sems, p_far, q_sems, q_far,
    a_send, a_recv, ag_send, ag_recv, g_send, g_recv, gq_send, gq_recv, d_send, d_recv,
):
    ver = lax.axis_index("ver")
    fsdp = lax.axis_index("fsdp")
    tp = lax.axis_index("tp")
    y, z = lax.div(fsdp, NZ), lax.rem(fsdp, NZ)
    half = NZ // 2
    trains, queries = train_acts.shape[1], query_acts.shape[1]
    count = trains + queries
    seq = train_acts.shape[2]
    tokens = count * seq

    def at_z(zz):
        return {"fsdp": y * NZ + zz}

    def at_y(d):
        return {"fsdp": lax.rem(y + d, ny) * NZ + z}

    def at_tp(d):
        return {"tp": lax.rem(tp + d, ntp)}

    def at_ver(v, d):
        return {"ver": lax.rem(ver + v, nver), "tp": lax.rem(tp + d, ntp)}

    tp_order = sorted(range(1, ntp), key=lambda d: abs(d - ntp // 2))
    y_order = sorted(range(1, ny), key=lambda d: abs(d - ny // 2))
    ver_order = [(v, d) for v in range(1, nver) for d in tp_order + [0]]
    zhalf, zpos = lax.div(z, half), lax.rem(z, half)
    other_z = [(1 - zhalf) * half + j for j in range(half)]
    same_z = [zhalf * half + lax.rem(zpos + i, half) for i in range(1, half)]

    def push(src, dst, send, recv, where):
        copy = pltpu.make_async_remote_copy(
            src_ref=src, dst_ref=dst, send_sem=send, recv_sem=recv, device_id=where, device_id_type=MESH
        )
        copy.start()

    def wait(ref, sem):
        pltpu.make_async_copy(ref, ref, sem).wait()

    load_pout = pltpu.make_async_copy(proj_out, pout, load_sem.at[0])
    load_pout.start()
    barrier = pltpu.get_barrier_semaphore()
    partners = [at_z(zz) for zz in other_z] + [at_y(d) for d in y_order[:3]]
    partners += [at_ver(v, d) for v, d in ver_order] + [at_tp(d) for d in tp_order[:3]]
    partners += [at_y(d) for d in y_order[3:]] + [at_z(zz) for zz in same_z] + [at_tp(d) for d in tp_order[3:]]
    for where in partners:
        pl.semaphore_signal(barrier, inc=1, device_id=where, device_id_type=MESH)
    loads_a = [
        pltpu.make_async_copy(proj_in, pin, load_sem.at[1]),
        pltpu.make_async_copy(train_acts.at[0], acts.at[pl.ds(0, trains)], load_sem.at[2]),
        pltpu.make_async_copy(query_acts.at[0], acts.at[pl.ds(trains, queries)], load_sem.at[3]),
    ]
    loads_g = [
        pltpu.make_async_copy(train_grads.at[0], grads.at[pl.ds(0, trains)], load_sem.at[4]),
        pltpu.make_async_copy(query_grads.at[0], grads.at[pl.ds(trains, queries)], load_sem.at[5]),
    ]
    load_step = pltpu.make_async_copy(step_size, step, load_sem.at[6])
    for load in loads_a + loads_g + [load_step]:
        load.start()

    near, far = pl.ds(1, half - 1), pl.ds(half, half)
    opposite = lax.rem(y + ny // 2, ny)

    def gather_own(buf, sems, far_recv):
        push(buf.at[y, 0], buf.at[y, 0], sems.at[1], far_recv.at[0], at_y(y_order[0]))
        for zz in other_z:
            push(buf.at[y, 0], buf.at[y, half + zpos], sems.at[0], sems.at[4], at_z(zz))
        for d in y_order[1:]:
            push(buf.at[y, 0], buf.at[y, 0], sems.at[1], sems.at[5], at_y(d))

    def gather_rest(buf, sems, far_recv):
        wait(buf.at[opposite, 0], far_recv.at[0])
        for zz in other_z:
            push(buf.at[opposite, 0], buf.at[opposite, half + zpos], sems.at[0], far_recv.at[y_order[0]], at_z(zz))
        wait(buf.at[pl.ds(0, ny - 2), 0], sems.at[5])
        for i, zz in enumerate(same_z):
            push(buf.at[:, 0], buf.at[:, half - 1 - i], sems.at[2], sems.at[6], at_z(zz))
        wait(buf.at[y, far], sems.at[4])
        for d in y_order[1:]:
            push(buf.at[y, far], buf.at[y, far], sems.at[3], far_recv.at[d], at_y(d))

    def gather_sent(buf, sems):
        wait(buf.at[pl.ds(0, 2), far], sems.at[0])
        wait(buf.at[pl.ds(0, ny - 1), 0], sems.at[1])
        wait(buf.at[:, near], sems.at[2])
        wait(buf.at[pl.ds(0, ny - 2), far], sems.at[3])

    slots = [
        jnp.where(k // half == zhalf, lax.rem(k % half - zpos + half, half), half + k % half) for k in range(NZ)
    ]

    load_pout.wait()
    own = pout[...].astype(F32)
    rank = own.shape[0]
    pbuf[y, 0] = jnp.concatenate([own[: rank // 2], own[rank // 2 :]], axis=1).astype(BF16)

    for load in loads_a:
        load.wait()
    a_part = lax.dot_general(pin[...], acts[...].reshape(tokens, -1), NT, preferred_element_type=F32)
    at_part[...] = a_part.reshape(at_part.shape)
    pl.semaphore_wait(barrier, len(partners))
    gather_own(pbuf, p_sems, p_far)

    for d in tp_order:
        push(at_part.at[(tp + d) % ntp], at_recv.at[d - 1], a_send, a_recv, at_tp(d))

    lane = lax.broadcasted_iota(jnp.int32, (rank // 2, 2 * rank), 1)
    is_left = lane < rank

    def place_row(row):
        cols = []
        for p in range(half):
            even = pbuf[row, slots[2 * p]].astype(F32)
            odd = pbuf[row, slots[2 * p + 1]].astype(F32)
            low = jnp.where(is_left, even, pltpu.roll(odd, rank, 1)).astype(BF16)
            high = jnp.where(is_left, pltpu.roll(even, rank, 1), odd).astype(BF16)
            cols.append(jnp.concatenate([low, high, low, high], axis=0))
        width = NZ * rank
        columns = pl.ds(pl.multiple_of(row * width, 128), width)
        pfull[:, columns] = jnp.concatenate(cols, axis=1)

    gather_rest(pbuf, p_sems, p_far)
    for load in loads_g + [load_step]:
        load.wait()
    wait(at_recv, a_recv)
    mine = at_part[tp]
    for d in range(ntp - 1):
        mine = mine + at_recv[d]
    at_full[tp] = mine
    for d in tp_order:
        push(at_full.at[tp], at_full.at[tp], ag_send, ag_recv, at_tp(d))

    wait(pbuf.at[:, near], p_sems.at[6])
    place_row(y)
    for d in reversed(y_order):
        row = lax.rem(y + ny - d, ny)
        wait(pbuf.at[row, far], p_far.at[d])
        place_row(row)
    g = grads[trains:].reshape(queries * seq, -1)
    bsum[trains * seq :, :] = lax.dot_general(g, pfull[...], NT, preferred_element_type=F32)

    wait(at_full.at[pl.ds(0, ntp - 1)], ag_recv)
    lanes2 = lax.broadcasted_iota(jnp.int32, (seq, 2 * rank), 1) < rank
    rows = rank // 2 // ntp

    def grad_parts(n, parts, at_row):
        at = at_full[:, :, n * seq : (n + 1) * seq].reshape(rank, seq)
        a_hi, a_lo = split(jnp.concatenate([at[: rank // 2], at[rank // 2 :]], axis=1))
        b = bsum[n * seq : (n + 1) * seq, :]
        b_hi, b_lo = split(jnp.concatenate([jnp.where(lanes2, b, 0.0), jnp.where(lanes2, 0.0, b)], axis=0))
        both = jnp.dot(jnp.concatenate([a_hi, a_lo], axis=0), b_hi, preferred_element_type=F32)
        grad = both[: rank // 2] + (both[rank // 2 :] + jnp.dot(a_hi, b_lo, preferred_element_type=F32))
        for t in range(ntp):
            parts[t, at_row : at_row + rows, :] = grad[t * rows : (t + 1) * rows, :]

    grad_parts(trains, gq, 0)
    for d in tp_order:
        push(gq.at[lax.rem(tp + d, ntp)], gqrecv.at[d - 1], gq_send, gq_recv, at_tp(d))
    g = grads[:trains].reshape(trains * seq, -1)
    bsum[: trains * seq, :] = lax.dot_general(g, pfull[...], NT, preferred_element_type=F32)
    for n in range(trains):
        grad_parts(n, gp, n * rows)
    for d in tp_order:
        push(gp.at[lax.rem(tp + d, ntp)], grecv.at[d - 1], g_send, g_recv, at_tp(d))
    wait(gqrecv, gq_recv)
    query = gq[tp]
    for d in range(ntp - 1):
        query = query + gqrecv[d]

    qbuf[y, 0] = query
    gather_own(qbuf, q_sems, q_far)
    gather_rest(qbuf, q_sems, q_far)
    wait(grecv, g_recv)
    grad = gp[tp]
    for d in range(ntp - 1):
        grad = grad + grecv[d]
    wait(qbuf.at[:, near], q_sems.at[6])
    for d in [0] + y_order[::-1]:
        row = lax.rem(y + ny - d, ny)
        if d:
            wait(qbuf.at[row, far], q_far.at[d])
        for k in range(NZ):
            crow[row, k * rows : (k + 1) * rows, :] = qbuf[row, slots[k]]

    wide = ny * NZ * rows
    q_hi, q_lo = split(crow[...].reshape(wide, 2 * rank))
    t_hi, t_lo = split(grad)
    many = trains * rows
    both = lax.dot_general(jnp.concatenate([t_hi, t_lo], axis=0), q_hi, NT, preferred_element_type=F32)
    cross = both[:many] + (both[many:] + lax.dot_general(t_hi, q_lo, NT, preferred_element_type=F32))
    row_id = lax.broadcasted_iota(jnp.int32, (many, wide), 0) % rows
    col_id = lax.broadcasted_iota(jnp.int32, (many, wide), 1) % rows
    cross = jnp.where(row_id == col_id, cross, 0.0)
    c_hi, c_rest = cross.astype(BF16), cross
    c_rest = c_rest - c_hi.astype(F32)
    c_mid, c_lo = split(c_rest)
    pick_from = lax.broadcasted_iota(jnp.int32, (wide, 128), 0) // rows
    pick_to = lax.broadcasted_iota(jnp.int32, (wide, 128), 1)
    pick = jnp.where(pick_from == pick_to, 1.0, 0.0).astype(BF16)
    three = jnp.dot(jnp.concatenate([c_hi, c_mid, c_lo], axis=0), pick, preferred_element_type=F32)
    part = three[:many] + (three[many : 2 * many] + three[2 * many :])
    me = ver * ntp + tp
    dbuf[me] = part * (step[0] / (seq * seq))

    targets = [{"ver": 0, "tp": lax.rem(tp + d, ntp)} for d in tp_order] + [at_ver(v, 0) for v in range(1, nver)]
    targets += [{"ver": v, "tp": lax.rem(tp + d, ntp)} for v in range(1, nver) for d in tp_order]
    for where in targets:
        push(dbuf.at[me], dbuf.at[me], d_send, d_recv, where)
    wait(dbuf.at[pl.ds(0, nver * ntp - 1)], d_recv)
    total = dbuf[0]
    for i in range(1, nver * ntp):
        total = total + dbuf[i]
    width = out.shape[1]
    for n in range(trains):
        out[n : n + 1, :] = jnp.sum(total[n * rows : (n + 1) * rows, :], axis=0, keepdims=True)[:, :width]

    gather_sent(pbuf, p_sems)
    gather_sent(qbuf, q_sems)
    wait(at_recv, a_send)
    wait(at_recv, ag_send)
    wait(grecv, g_send)
    wait(gqrecv, gq_send)
    wait(dbuf.at[pl.ds(0, nver * ntp - 1)], d_send)


def solution(mesh):
    nver, nfsdp, ntp = mesh.shape["ver"], mesh.shape["fsdp"], mesh.shape["tp"]
    ny = nfsdp // NZ

    def body(train_acts, train_grads, query_acts, query_grads, proj_in, proj_out, step_sizes):
        rank, din = proj_in.shape
        trains, queries = train_acts.shape[1], query_acts.shape[1]
        count, seq = trains + queries, train_acts.shape[2]
        tokens, dout = count * seq, train_grads.shape[3]
        arows = rank // ntp
        rows = rank // 2 // ntp
        dma = pltpu.SemaphoreType.DMA
        hbm = pl.BlockSpec(memory_space=pl.ANY)
        return pl.pallas_call(
            functools.partial(kernel, nver, ny, ntp),
            out_shape=jax.ShapeDtypeStruct((trains, nfsdp * queries), F32),
            in_specs=[hbm] * 7,
            out_specs=pl.BlockSpec(memory_space=pltpu.VMEM),
            scratch_shapes=[
                pltpu.VMEM((count, seq, din), BF16),
                pltpu.VMEM((count, seq, dout), BF16),
                pltpu.VMEM((rank, din), BF16),
                pltpu.VMEM(proj_out.shape, BF16),
                pltpu.VMEM((ny, NZ, rank // 2, 2 * proj_out.shape[1]), BF16),
                pltpu.VMEM((ntp, arows, tokens), F32),
                pltpu.VMEM((ntp - 1, arows, tokens), F32),
                pltpu.VMEM((ntp, arows, tokens), F32),
                pltpu.VMEM((2 * rank, dout), BF16),
                pltpu.VMEM((tokens, 2 * rank), F32),
                pltpu.VMEM((ntp, trains * rows, 2 * rank), F32),
                pltpu.VMEM((ntp - 1, trains * rows, 2 * rank), F32),
                pltpu.VMEM((ntp, queries * rows, 2 * rank), F32),
                pltpu.VMEM((ntp - 1, queries * rows, 2 * rank), F32),
                pltpu.VMEM((ny, NZ, rows, 2 * rank), F32),
                pltpu.VMEM((ny, NZ * rows, 2 * rank), F32),
                pltpu.VMEM((nver * ntp, trains * rows, 128), F32),
                pltpu.SMEM((1,), F32),
                dma((7,)), dma((7,)), dma((ny,)), dma((7,)), dma((ny,)),
                dma, dma, dma, dma, dma, dma, dma, dma, dma, dma,
            ],
            compiler_params=pltpu.CompilerParams(
                collective_id=0, has_side_effects=True, vmem_limit_bytes=56550000
            ),
        )(train_acts, train_grads, query_acts, query_grads, proj_in, proj_out, step_sizes)

    in_specs = (
        P("ver", "fsdp", None, "tp"),
        P("ver", "fsdp", None, "tp"),
        P("ver", "fsdp", None, "tp"),
        P("ver", "fsdp", None, "tp"),
        P(None, "tp"),
        P(None, ("tp", "fsdp")),
        P("ver"),
    )
    return jax.shard_map(body, mesh=mesh, in_specs=in_specs, out_specs=P("fsdp", None), check_vma=False)
```
